256 devices in a mesh: tm: 32 (over z_lo, x, core), gz: 8 (over z_hi, y).
Axes of the slice: x: 4, y: 4, z: 8 (z_hi: 2, z_lo: 4; z = z_hi * 4 + z_lo), core: 2. Of those that a mesh axis runs over, the one named last changes fastest.
Arguments:
- iterate: float32 [32, 128, 128, 256], P('tm', 'gz'), may hold values from -6 to 6
- initial: float32 [128, 128, 256], P('gz'), may hold values from -6 to 6
Outputs:
- updated: float32 [32, 128, 128, 256], P('tm', 'gz')
The draws below stay inside these ranges and needn't reach their ends.
All inputs are finite; a program needn't handle non-finite values.
Results may differ from the reference program's by a relative error of at most 0.0013.
Values sent between devices are 32-bit elements; how exact they have to be, the bound alone decides.
A program may use at most 128 MiB of HBM per device.

```python
import math
import jax
import jax.numpy as jnp
from jax import lax

NX = 256
NY = 128
NZ = 128
L = 32


def block_levels(stream_key, extent, cuts, low, largest):
    def one(dim, blocks):
        draws = jax.random.uniform(jax.random.fold_in(jax.random.fold_in(stream_key, 6), dim), (blocks,), jnp.float32, low / len(cuts), largest / len(cuts))
        return jnp.repeat(jnp.exp(draws), extent[dim] // blocks).reshape((-1,) + (1,) * (len(extent) - dim - 1))

    factor_of = one(*cuts[0])
    for cut in cuts[1:]:
        factor_of = factor_of * one(*cut)
    return factor_of


def gaussian(key, shape, spread, limit, shards=(), kind=jnp.bfloat16):
    array = jax.random.normal(key, shape, jnp.float32) * spread
    if len(shards) > 0:
        array = block_levels(key, shape, shards, -0.22, 0.18) * array
    return jnp.clip(array, min=-limit, max=limit).astype(kind)


def setup_inputs(seed: int = 0) -> dict:
    arg_keys = jax.random.split(jax.random.key(seed), 3)
    iterate = gaussian(arg_keys[0], (L, NZ, NY, NX), 1.0, 6.0, ((0, 32), (1, 8)), jnp.float32)
    initial = gaussian(arg_keys[1], (NZ, NY, NX), 1.0, 6.0, ((0, 8),), jnp.float32)
    return {"iterate": iterate, "initial": initial}


TIME_STEP = 0.05
DIFFUSION = 200.0
ALPHA_WEIGHT = 0.05
STABILIZER = 2.0


def symbol(length):
    positions = jnp.arange(length).astype(jnp.float32)
    return 2.0 * jnp.cos(positions * (2.0 * math.pi / length)) - 2.0


def reference(iterate, initial):
    earlier = jnp.concatenate([initial[None], iterate[:-1]], axis=0)
    laplace = -6.0 * iterate
    for dim_id in (1, 2, 3):
        laplace = laplace + jnp.roll(iterate, 1, dim_id) + jnp.roll(iterate, -1, dim_id)
    residual = earlier - iterate + TIME_STEP * (DIFFUSION * laplace + iterate - iterate * iterate * iterate)
    window = jnp.arange(L).astype(jnp.float32)
    damping = jnp.power(jnp.float32(ALPHA_WEIGHT), window / L)
    spectra = jnp.fft.fft(residual * damping[:, None, None, None], axis=0)
    root = ALPHA_WEIGHT ** (1.0 / L)
    angles = window * (2.0 * math.pi / L)
    den_re = 1.0 - root * jnp.cos(angles)
    den_im = root * jnp.sin(angles)
    total = symbol(NZ)[:, None, None] + symbol(NY)[None, :, None] + symbol(NX)[None, None, :]
    offset = TIME_STEP * (STABILIZER - DIFFUSION * total)

    def one_freq(packed):
        plane, shift_re, shift_im = packed
        solved = jnp.fft.fftn(plane) / ((shift_re + offset) + 1j * shift_im)
        return jnp.fft.ifftn(solved)

    solved = lax.map(one_freq, (spectra, den_re, den_im))
    correction = jnp.real(jnp.fft.ifft(solved, axis=0))
    return iterate + correction / damping[:, None, None, None]
```

```python
import functools
import math

import jax
import jax.numpy as jnp
import ml_dtypes
import numpy as np
from jax import lax
from jax.experimental import pallas as pl
from jax.experimental.pallas import tpu as pltpu
from jax.sharding import PartitionSpec as P

MESH = pl.DeviceIdType.MESH
F32 = jnp.float32
BF16 = jnp.bfloat16

NX, NY, NZ, L = 256, 128, 128, 32
TIME_STEP, DIFFUSION, ALPHA, STABILIZER = 0.05, 200.0, 0.05, 2.0
COUPLING = TIME_STEP * DIFFUSION
BLOCK = 8
SLABS = 4
HALF = NZ // 2
PLANES = 16
ROWS = 4
SETS = 2
KS = ROWS // SETS
ZROWS = 16


def real_basis(n):
    pos = np.arange(n)
    rows, freq = [np.ones(n) / math.sqrt(n), np.cos(math.pi * pos) / math.sqrt(n)], [0, n // 2]
    for m in range(1, n // 2):
        rows += [np.cos(2 * math.pi * m * pos / n) * math.sqrt(2 / n)]
        rows += [np.sin(2 * math.pi * m * pos / n) * math.sqrt(2 / n)]
        freq += [m, m]
    return np.stack(rows), 2.0 - 2.0 * np.cos(2 * math.pi * np.array(freq) / n)


def parts(m):
    m = np.asarray(m, np.float32)
    hi = m.astype(ml_dtypes.bfloat16)
    return hi, (m - hi.astype(np.float32)).astype(ml_dtypes.bfloat16)


def left(m):
    hi, lo = parts(m)
    return np.concatenate([hi, lo, hi], axis=1)


def right(m):
    hi, lo = parts(m)
    return np.concatenate([hi, lo, hi], axis=0)


def wide(column):
    return np.broadcast_to(np.asarray(column, np.float32)[:, None], (len(column), 128)).copy()


def tables():
    bx, lx = real_basis(NX)
    by, ly = real_basis(NY)
    bz, lz = real_basis(NZ)
    k = np.arange(1, HALF + 1)
    sine = np.sin(math.pi * np.outer(k, k) / (HALF + 1)) * math.sqrt(2 / (HALF + 1))
    lk = 2.0 - 2.0 * np.cos(math.pi * k / (HALF + 1))
    sign = np.where((np.arange(NZ) // 2) % 2 == 0, 1.0, -1.0)
    base = 1.0 + TIME_STEP * STABILIZER
    return dict(
        bx_f=right(bx.T),
        by_f=left(by),
        bx_i=right(bx),
        by_i=left(by.T),
        bz_s=left(np.concatenate([bz[:, :HALF], sine], axis=0)),
        bz_f=left(bz[:, :HALF]),
        bz_i=left(sine @ bz[:, :HALF].T),
        sine=left(sine),
        lxy=(base + COUPLING * (ly[:, None] + lx[None, :])).astype(np.float32),
        lz=wide(COUPLING * lz),
        lk=wide(COUPLING * lk),
        sign=wide(sign),
        edges=np.stack([wide(bz[:, p]) for p in (HALF - 1, 0, NZ - 1, HALF)]),
        walls=np.stack([wide(COUPLING * sine[:, 0]), wide(COUPLING * sine[:, HALF - 1])]),
    )


TABLES = tables()
NAMES = sorted(TABLES)


def split(x):
    hi = x.astype(BF16)
    return hi, (x - hi.astype(F32)).astype(BF16)


def dot(a, b):
    return jnp.dot(a, b, preferred_element_type=F32)


def dot_left(table, x):
    hi, lo = split(x)
    return dot(table, jnp.concatenate([hi, hi, lo], axis=0))


def dot_right(x, table):
    hi, lo = split(x)
    return dot(jnp.concatenate([hi, hi, lo], axis=1), table)


def twice(x):
    return jnp.concatenate([x, x], axis=1)


def drain(ref, sem):
    pltpu.make_async_copy(ref, ref, sem).wait()


def kernel(u_ref, init_ref, *refs):
    tab = dict(zip(NAMES, refs[: len(NAMES)]))
    (out_ref, u, s, sp, r, pb, sq, ys, yr, es, ec, er, fs, p, ws, s2,
     usem, isem, bsend, brecv, psend, precv, dsend, drecv, esend, erecv, fsend, frecv, hsend, hrecv) = refs[len(NAMES):]
    tm, gz = lax.axis_index("tm"), lax.axis_index("gz")
    block, step = tm // BLOCK, tm % BLOCK
    half, slab = gz // SLABS, gz % SLABS
    place = step * SLABS + slab
    ring = block * 2 + half

    load = pltpu.make_async_copy(u_ref.at[0], u, usem)
    load.start()

    def plane_peer(i):
        t, y = (step + i % BLOCK) % BLOCK, (slab + i // BLOCK) % SLABS
        return t, y, (block * BLOCK + t, half * SLABS + y)

    def ring_peer(i):
        to_b, to_h = (block + i % 4) % 4, (half + i // 4) % 2
        return to_b, to_h, (to_b * BLOCK + step, to_h * SLABS + slab)

    barrier = pltpu.get_barrier_semaphore()

    def greet_plane(i, c):
        pl.semaphore_signal(barrier, inc=1, device_id=plane_peer(i)[2], device_id_type=MESH)
        return c

    def greet_ring(i, c):
        pl.semaphore_signal(barrier, inc=1, device_id=ring_peer(i)[2], device_id_type=MESH)
        return c

    lax.fori_loop(1, 32, greet_plane, 0)
    lax.fori_loop(1, 8, greet_ring, 0)
    load.wait()

    def forward(x, dst, z):
        rows = dot_right(x.reshape(4 * NY, NX), tab["bx_f"][...])
        for i in range(4):
            dst[:, z + i, :] = dot_left(tab["by_f"][...], rows[i * NY:(i + 1) * NY])

    for g in range(PLANES // 4):
        x = u[4 * g:4 * g + 4]
        forward(x * (TIME_STEP * (STABILIZER + 1.0) - TIME_STEP * x * x), s, 4 * g)
    pl.semaphore_wait(barrier, 38)

    def send_b(i, c, k):
        t, y, dev = plane_peer(i)
        pltpu.make_async_remote_copy(
            src_ref=s.at[pl.ds((t * SLABS + y) * ROWS + k * KS, KS)],
            dst_ref=r.at[k, step, :, pl.ds(pl.multiple_of(slab * PLANES, PLANES), PLANES), :],
            send_sem=bsend.at[k], recv_sem=brecv.at[k], device_id=dev, device_id_type=MESH,
        ).start()
        return c

    for k in range(SETS):
        lax.fori_loop(1, 32, functools.partial(send_b, k=k), 0)
        pltpu.make_async_copy(
            s.at[pl.ds(place * ROWS + k * KS, KS)],
            r.at[k, step, :, pl.ds(pl.multiple_of(slab * PLANES, PLANES), PLANES), :],
            brecv.at[k],
        ).start()

    @pl.when(tm == L - 1)
    def _():
        load2 = pltpu.make_async_copy(init_ref, out_ref.at[0], isem)
        load2.start()
        load2.wait()
        for g in range(PLANES // 4):
            forward(out_ref[0, 4 * g:4 * g + 4] * (1.0 / ALPHA) - u[4 * g:4 * g + 4], sp, 4 * g)

        def send_p(i, c):
            t, y, dev = plane_peer(i)
            pltpu.make_async_remote_copy(
                src_ref=sp.at[pl.ds((t * SLABS + y) * ROWS, ROWS)],
                dst_ref=pb.at[:, pl.ds(pl.multiple_of(slab * PLANES, PLANES), PLANES), :],
                send_sem=psend, recv_sem=precv, device_id=dev, device_id_type=MESH,
            ).start()
            return c

        lax.fori_loop(1, 32, send_p, 0)
        pltpu.make_async_copy(
            sp.at[pl.ds(place * ROWS, ROWS)],
            pb.at[:, pl.ds(pl.multiple_of(slab * PLANES, PLANES), PLANES), :],
            precv,
        ).start()

    def decay(k, j, table):
        row = tab["lxy"][pl.ds(place * ROWS + k * KS + j, 1), :]
        return 1.0 / (row + twice(table))

    def stage_c(k):
        drain(r.at[k], brecv.at[k])
        if k == 0:
            @pl.when(block == 3)
            def _():
                drain(pb, precv)

        def one(j, c):
            a = decay(k, j, tab["lz"][...])
            z = None
            edges = [twice(tab["edges"][e]) for e in range(4)]
            for t in range(BLOCK):
                both = dot_left(tab["bz_s"][...], r[k, t, j])
                sq[k, t, j] = both[NZ:]
                z = a * both[:NZ] if z is None else a * (both[:NZ] + z)
                for e in range(4):
                    row = jnp.sum(z * edges[e], axis=0, keepdims=True)
                    if e < 2:
                        es[k, j, pl.ds(2 * t + e, 1), :] = row
                    else:
                        ec[k, j, pl.ds(2 * t + e - 2, 1), :] = row
            ys[k, j] = z
            return c

        lax.fori_loop(0, KS, one, 0)

        @pl.when(block == 3)
        def _():
            def add(j, c):
                ys[k, j] += dot_left(tab["bz_f"][...], pb[k * KS + j])
                return c
            lax.fori_loop(0, KS, add, 0)

        def send_d(i, c):
            to_b, to_h, dev = ring_peer(i)
            pltpu.make_async_remote_copy(
                src_ref=ys.at[k, :, pl.ds(pl.multiple_of((to_b * 2 + to_h) * ZROWS, ZROWS), ZROWS), :],
                dst_ref=yr.at[k, ring],
                send_sem=dsend.at[k], recv_sem=drecv.at[k], device_id=dev, device_id_type=MESH,
            ).start()
            return c

        lax.fori_loop(1, 8, send_d, 0)
        pltpu.make_async_copy(
            ys.at[k, :, pl.ds(pl.multiple_of(ring * ZROWS, ZROWS), ZROWS), :], yr.at[k, ring], drecv.at[k]
        ).start()
        pltpu.make_async_remote_copy(
            src_ref=es.at[k], dst_ref=er.at[k], send_sem=esend.at[k], recv_sem=erecv.at[k],
            device_id=ring_peer(4)[2], device_id_type=MESH,
        ).start()

    def stage_e(k):
        drain(yr.at[k], drecv.at[k])
        lz = tab["lz"][pl.ds(pl.multiple_of(ring * ZROWS, ZROWS), ZROWS), :]
        sign = twice(tab["sign"][0:ZROWS])
        for j in range(KS):
            a = decay(k, j, lz)
            g = a * a
            g = g * g
            g = g * g
            ends = [yr[k, 2 * b, j] + sign * yr[k, 2 * b + 1, j] for b in range(4)]
            total = ends[0]
            for b in range(1, 4):
                total = ends[b] + g * total
            g4 = g * g
            g4 = g4 * g4
            prev = total * (ALPHA / (1.0 - ALPHA * g4))
            for b in range(4):
                fs[k, b, j] = prev
                prev = ends[b] + g * prev

        def send_f(i, c):
            to_b, to_h, dev = ring_peer(i)
            pltpu.make_async_remote_copy(
                src_ref=fs.at[k, to_b],
                dst_ref=p.at[k, :, pl.ds(pl.multiple_of(ring * ZROWS, ZROWS), ZROWS), :],
                send_sem=fsend.at[k], recv_sem=frecv.at[k], device_id=dev, device_id_type=MESH,
            ).start()
            return c

        lax.fori_loop(1, 8, send_f, 0)
        pltpu.make_async_copy(
            fs.at[k, block], p.at[k, :, pl.ds(pl.multiple_of(ring * ZROWS, ZROWS), ZROWS), :], frecv.at[k]
        ).start()

    def stage_g(k):
        drain(p.at[k], frecv.at[k])
        drain(er.at[k], erecv.at[k])
        mirrored = half.astype(F32)

        def one(j, c):
            a = decay(k, j, tab["lz"][...])
            ak = decay(k, j, tab["lk"][...])
            v = p[k, j] * twice(1.0 + mirrored * (tab["sign"][...] - 1.0))
            w = dot_left(tab["bz_i"][...], v)
            outer = [twice(tab["edges"][e]) for e in (2, 3)]
            walls = [twice(tab["walls"][e]) for e in range(2)]
            for t in range(BLOCK):
                v = v * a
                rhs = sq[k, t, j] + w
                for e in range(2):
                    row = jnp.sum(v * outer[e], axis=0, keepdims=True)
                    row = row + er[k, j, pl.ds(2 * t + e, 1), :] + ec[k, j, pl.ds(2 * t + e, 1), :]
                    rhs = rhs + walls[e] * row
                w = ak * rhs
                ws[k, t, j] = dot_left(tab["sine"][...], w)
            return c

        lax.fori_loop(0, KS, one, 0)

        def send_h(i, c):
            t, y, dev = plane_peer(i)
            pltpu.make_async_remote_copy(
                src_ref=ws.at[k, t, :, pl.ds(pl.multiple_of(y * PLANES, PLANES), PLANES), :],
                dst_ref=s2.at[pl.ds(place * ROWS + k * KS, KS)],
                send_sem=hsend, recv_sem=hrecv, device_id=dev, device_id_type=MESH,
            ).start()
            return c

        lax.fori_loop(1, 32, send_h, 0)
        pltpu.make_async_copy(
            ws.at[k, step, :, pl.ds(pl.multiple_of(slab * PLANES, PLANES), PLANES), :],
            s2.at[pl.ds(place * ROWS + k * KS, KS)],
            hrecv,
        ).start()

    if SETS == 1:
        order = [(stage_c, 0), (stage_e, 0), (stage_g, 0)]
    else:
        order = [(stage_c, 0), (stage_e, 0), (stage_c, 1), (stage_g, 0), (stage_e, 1), (stage_g, 1)]
    for stage, k in order:
        stage(k)

    drain(s2, hrecv)
    for g in range(PLANES // 4):
        cols = [dot_left(tab["by_i"][...], s2[:, 4 * g + i, :]) for i in range(4)]
        rows = dot_right(jnp.concatenate(cols, axis=0), tab["bx_i"][...])
        out_ref[0, 4 * g:4 * g + 4] = rows.reshape(4, NY, NX)

    for k in range(SETS):
        drain(s.at[pl.ds(0, 31 * KS)], bsend.at[k])
        drain(p.at[k, :, pl.ds(0, 7 * ZROWS), :], dsend.at[k])
        drain(es.at[k], esend.at[k])
        drain(p.at[k, :, pl.ds(0, 7 * ZROWS), :], fsend.at[k])
    drain(s2.at[pl.ds(0, 31 * ROWS)], hsend)

    @pl.when(tm == L - 1)
    def _():
        drain(sp.at[pl.ds(0, 31 * ROWS)], psend)


def body(iterate, initial):
    dma = pltpu.SemaphoreType.DMA
    vmem = pl.BlockSpec(memory_space=pltpu.VMEM)
    hbm = pl.BlockSpec(memory_space=pl.ANY)
    return pl.pallas_call(
        kernel,
        out_shape=jax.ShapeDtypeStruct(iterate.shape, F32),
        in_specs=[hbm, hbm] + [vmem] * len(NAMES),
        out_specs=vmem,
        scratch_shapes=[
            pltpu.VMEM((PLANES, NY, NX), F32),
            pltpu.VMEM((NY, PLANES, NX), F32),
            pltpu.VMEM((NY, PLANES, NX), F32),
            pltpu.VMEM((SETS, BLOCK, KS, HALF, NX), F32),
            pltpu.VMEM((ROWS, HALF, NX), F32),
            pltpu.VMEM((SETS, BLOCK, KS, HALF, NX), F32),
            pltpu.VMEM((SETS, KS, NZ, NX), F32),
            pltpu.VMEM((SETS, 8, KS, ZROWS, NX), F32),
            pltpu.VMEM((SETS, KS, 2 * BLOCK, NX), F32),
            pltpu.VMEM((SETS, KS, 2 * BLOCK, NX), F32),
            pltpu.VMEM((SETS, KS, 2 * BLOCK, NX), F32),
            pltpu.VMEM((SETS, 4, KS, ZROWS, NX), F32),
            pltpu.VMEM((SETS, KS, NZ, NX), F32),
            pltpu.VMEM((SETS, BLOCK, KS, HALF, NX), F32),
            pltpu.VMEM((NY, PLANES, NX), F32),
            dma, dma, dma((SETS,)), dma((SETS,)), dma, dma, dma((SETS,)), dma((SETS,)),
            dma((SETS,)), dma((SETS,)), dma((SETS,)), dma((SETS,)), dma, dma,
        ],
        compiler_params=pltpu.CompilerParams(
            collective_id=0, has_side_effects=True, vmem_limit_bytes=56 * 1024 * 1024
        ),
        cost_estimate=pl.CostEstimate(flops=4 * 10**9, bytes_accessed=6 * 2**20, transcendentals=0),
        name="paradiag",
    )(iterate, initial, *[jnp.asarray(TABLES[n]) for n in NAMES])


def solution(mesh):
    return jax.shard_map(
        body,
        mesh=mesh,
        in_specs=(P("tm", "gz", None, None), P("gz", None, None)),
        out_specs=P("tm", "gz", None, None),
        check_vma=False,
    )
```

```python
import functools
import math

import jax
import jax.numpy as jnp
import ml_dtypes
import numpy as np
from jax import lax
from jax.experimental import pallas as pl
from jax.experimental.pallas import tpu as pltpu
from jax.sharding import PartitionSpec as P

MESH = pl.DeviceIdType.MESH
F32 = jnp.float32
BF16 = jnp.bfloat16

NX, NY, NZ, L = 256, 128, 128, 32
TIME_STEP, DIFFUSION, ALPHA, STABILIZER = 0.05, 200.0, 0.05, 2.0
COUPLING = TIME_STEP * DIFFUSION
BLOCK = 8
SLABS = 4
HALF = NZ // 2
PLANES = 16
ROWS = 4
PLACES = 32
HELP = PLANES // 2
SETS = 4
KS = ROWS // SETS
ZROWS = 16


def real_basis(n):
    pos = np.arange(n)
    rows, freq = [np.ones(n) / math.sqrt(n), np.cos(math.pi * pos) / math.sqrt(n)], [0, n // 2]
    for m in range(1, n // 2):
        rows += [np.cos(2 * math.pi * m * pos / n) * math.sqrt(2 / n)]
        rows += [np.sin(2 * math.pi * m * pos / n) * math.sqrt(2 / n)]
        freq += [m, m]
    return np.stack(rows), 2.0 - 2.0 * np.cos(2 * math.pi * np.array(freq) / n)


def parts(m):
    m = np.asarray(m, np.float32)
    hi = m.astype(ml_dtypes.bfloat16)
    return hi, (m - hi.astype(np.float32)).astype(ml_dtypes.bfloat16)


def left(m):
    hi, lo = parts(m)
    return np.concatenate([hi, lo, hi], axis=1)


def right(m):
    hi, lo = parts(m)
    return np.concatenate([hi, lo, hi], axis=0)


def wide(column):
    return np.broadcast_to(np.asarray(column, np.float32)[:, None], (len(column), 128)).copy()


def tables():
    bx, lx = real_basis(NX)
    by, ly = real_basis(NY)
    bz, lz = real_basis(NZ)
    k = np.arange(1, HALF + 1)
    sine = np.sin(math.pi * np.outer(k, k) / (HALF + 1)) * math.sqrt(2 / (HALF + 1))
    lk = 2.0 - 2.0 * np.cos(math.pi * k / (HALF + 1))
    sign = np.where((np.arange(NZ) // 2) % 2 == 0, 1.0, -1.0)
    base = 1.0 + TIME_STEP * STABILIZER
    return dict(
        bx_f=right(bx.T),
        by_f=left(by),
        bx_i=right(bx),
        by_i=left(by.T),
        bz_s=left(np.concatenate([bz[:, :HALF], sine], axis=0)),
        bz_f=left(bz[:, :HALF]),
        bz_i=left(sine @ bz[:, :HALF].T),
        sine=left(sine),
        lxy=(base + COUPLING * (ly[:, None] + lx[None, :])).astype(np.float32),
        lz=wide(COUPLING * lz),
        lk=wide(COUPLING * lk),
        sign=wide(sign),
        edges=np.stack([wide(bz[:, p]) for p in (HALF - 1, 0, NZ - 1, HALF)]),
        walls=np.stack([wide(COUPLING * sine[:, 0]), wide(COUPLING * sine[:, HALF - 1])]),
    )


TABLES = tables()
NAMES = sorted(TABLES)


def split(x):
    hi = x.astype(BF16)
    return hi, (x - hi.astype(F32)).astype(BF16)


def dot(a, b):
    return jnp.dot(a, b, preferred_element_type=F32)


def dot_left(table, x):
    hi, lo = split(x)
    return dot(table, jnp.concatenate([hi, hi, lo], axis=0))


def dot_right(x, table):
    hi, lo = split(x)
    return dot(jnp.concatenate([hi, hi, lo], axis=1), table)


def twice(x):
    return jnp.concatenate([x, x], axis=1)


def drain(ref, sem):
    pltpu.make_async_copy(ref, ref, sem).wait()


def kernel(u_ref, init_ref, *refs):
    tab = dict(zip(NAMES, refs[: len(NAMES)]))
    (out_ref, u, ty, s, pa, hp, ph, sp, r, pb, sq, ys, yr, es, ec, er, fs, p, ws, s2,
     usem, isem, osem, bsend, brecv, rsend, rrecv, psend, precv,
     dsend, drecv, esend, erecv, fsend, frecv, hsend, hrecv) = refs[len(NAMES):]
    tm, gz = lax.axis_index("tm"), lax.axis_index("gz")
    block, step = tm // BLOCK, tm % BLOCK
    half, slab = gz // SLABS, gz % SLABS
    place = step * SLABS + slab
    ring = block * 2 + half
    last = tm == L - 1
    helper = jnp.logical_and(step == BLOCK - 1, block % 2 == 0)
    part = 1 - block // 2
    origin = jnp.where(block == 0, 1 - half, half)

    load = pltpu.make_async_copy(u_ref.at[0], u, usem)
    load.start()

    @pl.when(last)
    def _():
        pltpu.make_async_copy(init_ref, pa, isem).start()

    def plane_peer(i):
        t, y = (step + i // SLABS) % BLOCK, (slab + i % SLABS) % SLABS
        return t, y, (block * BLOCK + t, half * SLABS + y)

    def ring_peer(i):
        to_b, to_h = (block + i % 4) % 4, (half + i // 4) % 2
        return to_b, to_h, (to_b * BLOCK + step, to_h * SLABS + slab)

    barrier = pltpu.get_barrier_semaphore()

    def greet_plane(i, c):
        pl.semaphore_signal(barrier, inc=1, device_id=plane_peer(i)[2], device_id_type=MESH)
        return c

    def greet_ring(i, c):
        pl.semaphore_signal(barrier, inc=1, device_id=ring_peer(i)[2], device_id_type=MESH)
        return c

    lax.fori_loop(1, PLACES, greet_plane, 0)
    lax.fori_loop(1, 8, greet_ring, 0)

    @pl.when(block == 3)
    def _():
        for y in range(SLABS):
            for dev in ((2 * BLOCK + BLOCK - 1, half * SLABS + y), (BLOCK - 1, (1 - half) * SLABS + y)):
                pl.semaphore_signal(barrier, inc=1, device_id=dev, device_id_type=MESH)

    load.wait()

    def along_y(x, dst, z):
        for i in range(4):
            dst[:, z + i, :] = dot_left(tab["by_f"][...], x[i])

    def along_x(src, dst, k, planes):
        rows = src[pl.ds(k * PLACES * KS, PLACES * KS)].reshape(PLACES * KS * planes, NX)
        dst[pl.ds(k * PLACES * KS, PLACES * KS)] = dot_right(rows, tab["bx_f"][...]).reshape(PLACES * KS, planes, NX)

    @pl.when(last)
    def _():
        pltpu.make_async_copy(init_ref, pa, isem).wait()
        pa[...] = pa[...] * (1.0 / ALPHA) - u[...]

    @pl.when(helper)
    def _():
        pl.semaphore_wait(barrier, PLACES - 1 + 7 + PLACES)

    @pl.when(jnp.logical_not(helper))
    def _():
        pl.semaphore_wait(barrier, PLACES - 1 + 7)

    def raw(q, c):
        return pltpu.make_async_remote_copy(
            src_ref=pa.at[pl.ds(q * HELP + c * 4, 4)], dst_ref=hp.at[pl.ds(c * 4, 4)],
            send_sem=rsend.at[q, c], recv_sem=rrecv.at[c],
            device_id=((2 * BLOCK + BLOCK - 1, gz), (BLOCK - 1, (1 - half) * SLABS + slab))[q], device_id_type=MESH,
        )

    @pl.when(last)
    def _():
        for c in range(2):
            for q in range(2):
                raw(q, c).start()

    for g in range(PLANES // 4):
        x = u[4 * g:4 * g + 4]
        along_y(x * (TIME_STEP * (STABILIZER + 1.0) - TIME_STEP * x * x), ty, 4 * g)

    def send_b(i, c, k):
        t, y, dev = plane_peer(i)
        pltpu.make_async_remote_copy(
            src_ref=s.at[pl.ds((k * PLACES + t * SLABS + y) * KS, KS)],
            dst_ref=r.at[k, step, :, pl.ds(pl.multiple_of(slab * PLANES, PLANES), PLANES), :],
            send_sem=bsend.at[k], recv_sem=brecv.at[k], device_id=dev, device_id_type=MESH,
        ).start()
        return c

    def send_p(i, c, k):
        t, y = (step + i // SLABS) % BLOCK, (slab + i % SLABS) % SLABS
        pltpu.make_async_remote_copy(
            src_ref=sp.at[pl.ds((k * PLACES + t * SLABS + y) * KS, KS)],
            dst_ref=pb.at[k, :, pl.ds(pl.multiple_of(slab * PLANES + part * HELP, HELP), HELP), :],
            send_sem=psend.at[k], recv_sem=precv.at[k], device_id=(3 * BLOCK + t, origin * SLABS + y), device_id_type=MESH,
        ).start()
        return c

    for k in range(SETS):
        along_x(ty, s, k, PLANES)
        lax.fori_loop(1, PLACES, functools.partial(send_b, k=k), 0)
        pltpu.make_async_copy(
            s.at[pl.ds((k * PLACES + place) * KS, KS)],
            r.at[k, step, :, pl.ds(pl.multiple_of(slab * PLANES, PLANES), PLANES), :],
            brecv.at[k],
        ).start()

        @pl.when(helper)
        def _():
            if k == 0:
                for c in range(2):
                    drain(hp.at[pl.ds(c * 4, 4)], rrecv.at[c])
                    along_y(hp[4 * c:4 * c + 4], ph, 4 * c)
            along_x(ph, sp, k, HELP)
            lax.fori_loop(0, PLACES, functools.partial(send_p, k=k), 0)

    def decay(k, j, table):
        row = tab["lxy"][pl.ds((k * PLACES + place) * KS + j, 1), :]
        return 1.0 / (row + twice(table))

    def stage_c(k):
        drain(r.at[k], brecv.at[k])

        @pl.when(block == 3)
        def _():
            drain(pb.at[k], precv.at[k])

        def one(j, c):
            a = decay(k, j, tab["lz"][...])
            z = None
            edges = [twice(tab["edges"][e]) for e in range(4)]
            for t in range(BLOCK):
                both = dot_left(tab["bz_s"][...], r[k, t, j])
                sq[k, t, j] = both[NZ:]
                z = a * both[:NZ] if z is None else a * (both[:NZ] + z)
                for e in range(4):
                    row = jnp.sum(z * edges[e], axis=0, keepdims=True)
                    if e < 2:
                        es[k, j, pl.ds(2 * t + e, 1), :] = row
                    else:
                        ec[k, j, pl.ds(2 * t + e - 2, 1), :] = row
            ys[k, j] = z
            return c

        lax.fori_loop(0, KS, one, 0)

        @pl.when(block == 3)
        def _():
            def add(j, c):
                ys[k, j] += dot_left(tab["bz_f"][...], pb[k, j])
                return c
            lax.fori_loop(0, KS, add, 0)

        def send_d(i, c):
            to_b, to_h, dev = ring_peer(i)
            pltpu.make_async_remote_copy(
                src_ref=ys.at[k, :, pl.ds(pl.multiple_of((to_b * 2 + to_h) * ZROWS, ZROWS), ZROWS), :],
                dst_ref=yr.at[k, ring],
                send_sem=dsend.at[k], recv_sem=drecv.at[k], device_id=dev, device_id_type=MESH,
            ).start()
            return c

        lax.fori_loop(1, 8, send_d, 0)
        pltpu.make_async_copy(
            ys.at[k, :, pl.ds(pl.multiple_of(ring * ZROWS, ZROWS), ZROWS), :], yr.at[k, ring], drecv.at[k]
        ).start()
        pltpu.make_async_remote_copy(
            src_ref=es.at[k], dst_ref=er.at[k], send_sem=esend.at[k], recv_sem=erecv.at[k],
            device_id=ring_peer(4)[2], device_id_type=MESH,
        ).start()

    def stage_e(k):
        drain(yr.at[k], drecv.at[k])
        lz = tab["lz"][pl.ds(pl.multiple_of(ring * ZROWS, ZROWS), ZROWS), :]
        sign = twice(tab["sign"][0:ZROWS])
        for j in range(KS):
            a = decay(k, j, lz)
            g = a * a
            g = g * g
            g = g * g
            ends = [yr[k, 2 * b, j] + sign * yr[k, 2 * b + 1, j] for b in range(4)]
            total = ends[0]
            for b in range(1, 4):
                total = ends[b] + g * total
            g4 = g * g
            g4 = g4 * g4
            prev = total * (ALPHA / (1.0 - ALPHA * g4))
            for b in range(4):
                fs[k, b, j] = prev
                prev = ends[b] + g * prev

        def send_f(i, c):
            to_b, to_h, dev = ring_peer(i)
            pltpu.make_async_remote_copy(
                src_ref=fs.at[k, to_b],
                dst_ref=p.at[k, :, pl.ds(pl.multiple_of(ring * ZROWS, ZROWS), ZROWS), :],
                send_sem=fsend.at[k], recv_sem=frecv.at[k], device_id=dev, device_id_type=MESH,
            ).start()
            return c

        lax.fori_loop(1, 8, send_f, 0)
        pltpu.make_async_copy(
            fs.at[k, block], p.at[k, :, pl.ds(pl.multiple_of(ring * ZROWS, ZROWS), ZROWS), :], frecv.at[k]
        ).start()

    def stage_g(k):
        drain(p.at[k], frecv.at[k])
        drain(er.at[k], erecv.at[k])
        mirrored = half.astype(F32)

        def one(j, c):
            a = decay(k, j, tab["lz"][...])
            ak = decay(k, j, tab["lk"][...])
            v = p[k, j] * twice(1.0 + mirrored * (tab["sign"][...] - 1.0))
            w = dot_left(tab["bz_i"][...], v)
            outer = [twice(tab["edges"][e]) for e in (2, 3)]
            walls = [twice(tab["walls"][e]) for e in range(2)]
            for t in range(BLOCK):
                v = v * a
                rhs = sq[k, t, j] + w
                for e in range(2):
                    row = jnp.sum(v * outer[e], axis=0, keepdims=True)
                    row = row + er[k, j, pl.ds(2 * t + e, 1), :] + ec[k, j, pl.ds(2 * t + e, 1), :]
                    rhs = rhs + walls[e] * row
                w = ak * rhs
                ws[k, t, j] = dot_left(tab["sine"][...], w)
            return c

        lax.fori_loop(0, KS, one, 0)

        def send_h(i, c):
            t, y, dev = plane_peer(i)
            pltpu.make_async_remote_copy(
                src_ref=ws.at[k, t, :, pl.ds(pl.multiple_of(y * PLANES, PLANES), PLANES), :],
                dst_ref=s2.at[pl.ds((k * PLACES + place) * KS, KS)],
                send_sem=hsend, recv_sem=hrecv.at[k], device_id=dev, device_id_type=MESH,
            ).start()
            return c

        lax.fori_loop(1, 32, send_h, 0)
        pltpu.make_async_copy(
            ws.at[k, step, :, pl.ds(pl.multiple_of(slab * PLANES, PLANES), PLANES), :],
            s2.at[pl.ds((k * PLACES + place) * KS, KS)],
            hrecv.at[k],
        ).start()

    for k in range(SETS):
        stage_c(k)
        if k > 0:
            stage_g(k - 1)
        stage_e(k)
    stage_g(SETS - 1)

    for k in range(SETS):
        rows = pl.ds(k * PLACES * KS, PLACES * KS)
        drain(s2.at[rows], hrecv.at[k])
        x = dot_right(s2[rows].reshape(PLACES * KS * PLANES, NX), tab["bx_i"][...])
        ty[rows] = x.reshape(PLACES * KS, PLANES, NX)

    def store(g):
        return pltpu.make_async_copy(u.at[pl.ds(4 * g, 4)], out_ref.at[0, pl.ds(4 * g, 4)], osem.at[g])

    for g in range(PLANES // 4):
        for i in range(4):
            u[4 * g + i] = dot_left(tab["by_i"][...], ty[:, 4 * g + i, :])
        store(g).start()

    for k in range(SETS):
        drain(s.at[pl.ds(0, 31 * KS)], bsend.at[k])
        drain(p.at[k, :, pl.ds(0, 7 * ZROWS), :], dsend.at[k])
        drain(es.at[k], esend.at[k])
        drain(p.at[k, :, pl.ds(0, 7 * ZROWS), :], fsend.at[k])
    drain(s2.at[pl.ds(0, 31 * ROWS)], hsend)

    @pl.when(last)
    def _():
        for c in range(2):
            for q in range(2):
                drain(pa.at[pl.ds(0, 4)], rsend.at[q, c])

    @pl.when(helper)
    def _():
        for k in range(SETS):
            drain(sp.at[pl.ds(0, PLACES * KS)], psend.at[k])

    for g in range(PLANES // 4):
        store(g).wait()


def body(iterate, initial):
    dma = pltpu.SemaphoreType.DMA
    vmem = pl.BlockSpec(memory_space=pltpu.VMEM)
    hbm = pl.BlockSpec(memory_space=pl.ANY)
    return pl.pallas_call(
        kernel,
        out_shape=jax.ShapeDtypeStruct(iterate.shape, F32),
        in_specs=[hbm, hbm] + [vmem] * len(NAMES),
        out_specs=hbm,
        scratch_shapes=[
            pltpu.VMEM((PLANES, NY, NX), F32),
            pltpu.VMEM((NY, PLANES, NX), F32),
            pltpu.VMEM((NY, PLANES, NX), F32),
            pltpu.VMEM((PLANES, NY, NX), F32),
            pltpu.VMEM((HELP, NY, NX), F32),
            pltpu.VMEM((NY, HELP, NX), F32),
            pltpu.VMEM((NY, HELP, NX), F32),
            pltpu.VMEM((SETS, BLOCK, KS, HALF, NX), F32),
            pltpu.VMEM((SETS, KS, HALF, NX), F32),
            pltpu.VMEM((SETS, BLOCK, KS, HALF, NX), F32),
            pltpu.VMEM((SETS, KS, NZ, NX), F32),
            pltpu.VMEM((SETS, 8, KS, ZROWS, NX), F32),
            pltpu.VMEM((SETS, KS, 2 * BLOCK, NX), F32),
            pltpu.VMEM((SETS, KS, 2 * BLOCK, NX), F32),
            pltpu.VMEM((SETS, KS, 2 * BLOCK, NX), F32),
            pltpu.VMEM((SETS, 4, KS, ZROWS, NX), F32),
            pltpu.VMEM((SETS, KS, NZ, NX), F32),
            pltpu.VMEM((SETS, BLOCK, KS, HALF, NX), F32),
            pltpu.VMEM((NY, PLANES, NX), F32),
            dma, dma, dma((PLANES // 4,)),
            dma((SETS,)), dma((SETS,)), dma((2, 2)), dma((2,)), dma((SETS,)), dma((SETS,)),
            dma((SETS,)), dma((SETS,)), dma((SETS,)), dma((SETS,)), dma((SETS,)), dma((SETS,)),
            dma, dma((SETS,)),
        ],
        compiler_params=pltpu.CompilerParams(
            collective_id=0, has_side_effects=True, vmem_limit_bytes=56 * 1024 * 1024
        ),
        cost_estimate=pl.CostEstimate(flops=4 * 10**9, bytes_accessed=6 * 2**20, transcendentals=0),
        name="paradiag",
    )(iterate, initial, *[jnp.asarray(TABLES[n]) for n in NAMES])


def solution(mesh):
    return jax.shard_map(
        body,
        mesh=mesh,
        in_specs=(P("tm", "gz", None, None), P("gz", None, None)),
        out_specs=P("tm", "gz", None, None),
        check_vma=False,
    )
```

```python
import functools
import math

import jax
import jax.numpy as jnp
import ml_dtypes
import numpy as np
from jax import lax
from jax.experimental import pallas as pl
from jax.experimental.pallas import tpu as pltpu
from jax.sharding import PartitionSpec as P

MESH = pl.DeviceIdType.MESH
F32 = jnp.float32
BF16 = jnp.bfloat16

NX, NY, NZ, L = 256, 128, 128, 32
TIME_STEP, DIFFUSION, ALPHA, STABILIZER = 0.05, 200.0, 0.05, 2.0
COUPLING = TIME_STEP * DIFFUSION
BLOCK = 8
SLABS = 4
HALF = NZ // 2
PLANES = 16
ROWS = 4
PLACES = 32
HELP = 2
HELP_AFTER = 0
SETS = 4
KS = ROWS // SETS
ZROWS = 16


def peers():
    found = []
    for x in range(4):
        for core in range(2):
            for y in range(SLABS):
                for one in ((x, core, y), (-x % 4, core, -y % SLABS)):
                    if one not in found and one != (0, 0, 0):
                        found.append(one)
    return found


PEERS = peers()


def real_basis(n):
    pos = np.arange(n)
    rows, freq = [np.ones(n) / math.sqrt(n), np.cos(math.pi * pos) / math.sqrt(n)], [0, n // 2]
    for m in range(1, n // 2):
        rows += [np.cos(2 * math.pi * m * pos / n) * math.sqrt(2 / n)]
        rows += [np.sin(2 * math.pi * m * pos / n) * math.sqrt(2 / n)]
        freq += [m, m]
    return np.stack(rows), 2.0 - 2.0 * np.cos(2 * math.pi * np.array(freq) / n)


def parts(m):
    m = np.asarray(m, np.float32)
    hi = m.astype(ml_dtypes.bfloat16)
    return hi, (m - hi.astype(np.float32)).astype(ml_dtypes.bfloat16)


def left(m):
    hi, lo = parts(m)
    return np.concatenate([hi, lo, hi], axis=1)


def right(m):
    hi, lo = parts(m)
    return np.concatenate([hi, lo, hi], axis=0)


def wide(column):
    return np.broadcast_to(np.asarray(column, np.float32)[:, None], (len(column), 128)).copy()


def tables():
    bx, lx = real_basis(NX)
    by, ly = real_basis(NY)
    bz, lz = real_basis(NZ)
    k = np.arange(1, HALF + 1)
    sine = np.sin(math.pi * np.outer(k, k) / (HALF + 1)) * math.sqrt(2 / (HALF + 1))
    lk = 2.0 - 2.0 * np.cos(math.pi * k / (HALF + 1))
    sign = np.where((np.arange(NZ) // 2) % 2 == 0, 1.0, -1.0)
    base = 1.0 + TIME_STEP * STABILIZER
    return dict(
        bx_f=right(bx.T),
        by_f=left(by),
        bx_i=right(bx),
        by_i=left(by.T),
        bz_s=left(np.concatenate([bz[:, :HALF], sine], axis=0)),
        bz_p=left(bz[:, [i + HELP * n for i in range(HELP) for n in range(HALF // HELP)]]),
        bz_i=left(sine @ bz[:, :HALF].T),
        sine=left(sine),
        lxy=(base + COUPLING * (ly[:, None] + lx[None, :])).astype(np.float32),
        lz=wide(COUPLING * lz),
        lk=wide(COUPLING * lk),
        sign=wide(sign),
        edges=np.stack([wide(bz[:, p]) for p in (HALF - 1, 0, NZ - 1, HALF)]),
        walls=np.stack([wide(COUPLING * sine[:, 0]), wide(COUPLING * sine[:, HALF - 1])]),
    )


TABLES = tables()
NAMES = sorted(TABLES)


def split(x):
    hi = x.astype(BF16)
    return hi, (x - hi.astype(F32)).astype(BF16)


def dot(a, b):
    return jnp.dot(a, b, preferred_element_type=F32)


def dot_left(table, x):
    hi, lo = split(x)
    return dot(table, jnp.concatenate([hi, hi, lo], axis=0))


def dot_right(x, table):
    hi, lo = split(x)
    return dot(jnp.concatenate([hi, hi, lo], axis=1), table)


def twice(x):
    return jnp.concatenate([x, x], axis=1)


def drain(ref, sem):
    pltpu.make_async_copy(ref, ref, sem).wait()


def kernel(u_ref, init_ref, *refs):
    tab = dict(zip(NAMES, refs[: len(NAMES)]))
    (out_ref, u, ty, s, pa, hp, sp, r, pb, sq, ys, yr, es, ec, er, fs, p, ws, s2,
     usem, isem, osem, bsend, brecv, rsend, rrecv, psend, precv,
     dsend, drecv, esend, erecv, fsend, frecv, hsend, hrecv) = refs[len(NAMES):]
    tm, gz = lax.axis_index("tm"), lax.axis_index("gz")
    block, step = tm // BLOCK, tm % BLOCK
    half, slab = gz // SLABS, gz % SLABS
    place = step * SLABS + slab
    ring = block * 2 + half
    x, core = step // 2, step % 2
    last = tm == L - 1
    beside = jnp.logical_and(block == 3, jnp.logical_or(x % 2 == 0, step == BLOCK - 2))
    above = jnp.logical_and(x == 3, jnp.logical_or(block == 2, jnp.logical_and(block == 1, core == 0)))
    helper = jnp.logical_or(beside, above)
    part = jnp.where(block == 3, jnp.where(x == 3, 4, x + core), jnp.where(block == 2, 5 + core, 7))

    load = pltpu.make_async_copy(u_ref.at[0], u, usem)
    load.start()

    state = pltpu.make_async_copy(init_ref.at[pl.ds(part * HELP, HELP)], pa, isem)

    @pl.when(helper)
    def _():
        state.start()

    def plane_peer(one):
        dx, dc, dy = one
        t, y = (x + dx) % 4 * 2 + (core + dc) % 2, (slab + dy) % SLABS
        return t, y, (block * BLOCK + t, half * SLABS + y)

    def ring_peer(i):
        to_b, to_h = (block + i % 4) % 4, (half + i // 4) % 2
        return to_b, to_h, (to_b * BLOCK + step, to_h * SLABS + slab)

    barrier = pltpu.get_barrier_semaphore()

    def greet(dev):
        pl.semaphore_signal(barrier, inc=1, device_id=dev, device_id_type=MESH)

    for one in PEERS:
        greet(plane_peer(one)[2])
    for i in range(1, 8):
        greet(ring_peer(i)[2])

    @pl.when(block == 3)
    def _():
        for y in range(SLABS):
            for c in range(2):
                greet((2 * BLOCK + 6 + c, half * SLABS + y))
            greet((BLOCK + 6, half * SLABS + y))

    @pl.when(jnp.logical_and(above, core == 0))
    def _():
        greet((L - 1, gz))

    greeted = PLACES - 1 + 7

    @pl.when(last)
    def _():
        pl.semaphore_wait(barrier, greeted + 2)

    load.wait()

    @pl.when(last)
    def _():
        for c in range(4 * HELP):
            for q in (0, 2, 5, 4, 1, 3, 6, 7):
                where = (pl.ds(c // 4, 1), pl.ds(c % 4 * 32, 32))
                pltpu.make_async_remote_copy(
                    src_ref=u.at[pl.ds(q * HELP + c // 4, 1), where[1]], dst_ref=hp.at[where],
                    send_sem=rsend, recv_sem=rrecv,
                    device_id=((24, 25, 28, 29, 30, 22, 23, 14)[q], gz), device_id_type=MESH,
                ).start()


    def along_y(x, dst, z):
        for i in range(4):
            dst[:, z + i, :] = dot_left(tab["by_f"][...], x[i])

    def along_x(k):
        rows = pl.ds(k * PLACES * KS, PLACES * KS)
        done = dot_right(ty[rows].reshape(PLACES * KS * PLANES, NX), tab["bx_f"][...])
        s[rows] = done.reshape(PLACES * KS, PLANES, NX)

    for g in range(PLANES // 4):
        v = u[4 * g:4 * g + 4]
        along_y(v * (TIME_STEP * (STABILIZER + 1.0) - TIME_STEP * v * v), ty, 4 * g)

    @pl.when(above)
    def _():
        pl.semaphore_wait(barrier, greeted + PLACES)

    @pl.when(jnp.logical_not(jnp.logical_or(above, last)))
    def _():
        pl.semaphore_wait(barrier, greeted)

    def send_b(one, k):
        t, y, dev = plane_peer(one)
        pltpu.make_async_remote_copy(
            src_ref=s.at[pl.ds((k * PLACES + t * SLABS + y) * KS, KS)],
            dst_ref=r.at[k, step, :, pl.ds(pl.multiple_of(slab * PLANES, PLANES), PLANES), :],
            send_sem=bsend.at[k], recv_sem=brecv.at[k], device_id=dev, device_id_type=MESH,
        ).start()

    def send_p(one):
        t, y, _ = plane_peer(one)
        pltpu.make_async_remote_copy(
            src_ref=sp.at[t * SLABS + y], dst_ref=pb.at[slab * 8 + part],
            send_sem=psend, recv_sem=precv, device_id=(3 * BLOCK + t, half * SLABS + y), device_id_type=MESH,
        ).start()

    for k in range(SETS):
        along_x(k)
        for one in PEERS:
            send_b(one, k)
        pltpu.make_async_copy(
            s.at[pl.ds((k * PLACES + place) * KS, KS)],
            r.at[k, step, :, pl.ds(pl.multiple_of(slab * PLANES, PLANES), PLANES), :],
            brecv.at[k],
        ).start()
        if k != HELP_AFTER:
            continue


        @pl.when(helper)
        def _():
            state.wait()
            drain(hp, rrecv)
            rows = [dot_left(tab["by_f"][...], pa[i] * (1.0 / ALPHA) - hp[i]) for i in range(HELP)]
            rows = dot_right(jnp.concatenate(rows, axis=0), tab["bx_f"][...])
            for i in range(HELP):
                for m in range(ROWS):
                    sp[:, HELP * m + i, :] = rows[i * NY + m * PLACES:i * NY + (m + 1) * PLACES]
            for one in PEERS:
                send_p(one)

        @pl.when(beside)
        def _():
            pltpu.make_async_copy(sp.at[place], pb.at[slab * 8 + part], precv).start()

        @pl.when(above)
        def _():
            send_p((0, 0, 0))

    def decay(k, j, table):
        row = tab["lxy"][pl.ds((k * PLACES + place) * KS + j, 1), :]
        return 1.0 / (row + twice(table))

    def stage_c(k):
        drain(r.at[k], brecv.at[k])

        if k == 0:
            @pl.when(block == 3)
            def _():
                drain(pb, precv)

        def one(j, c):
            a = decay(k, j, tab["lz"][...])
            z = None
            edges = [twice(tab["edges"][e]) for e in range(4)]
            for t in range(BLOCK):
                both = dot_left(tab["bz_s"][...], r[k, t, j])
                sq[k, t, j] = both[NZ:]
                z = a * both[:NZ] if z is None else a * (both[:NZ] + z)
                for e in range(4):
                    row = jnp.sum(z * edges[e], axis=0, keepdims=True)
                    if e < 2:
                        es[k, j, pl.ds(2 * t + e, 1), :] = row
                    else:
                        ec[k, j, pl.ds(2 * t + e - 2, 1), :] = row
            ys[k, j] = z
            return c

        lax.fori_loop(0, KS, one, 0)

        @pl.when(block == 3)
        def _():
            def add(j, c):
                extra = [pb[:, HELP * k + i, :] for i in range(HELP)]
                ys[k, j] += dot_left(tab["bz_p"][...], jnp.concatenate(extra, axis=0))
                return c
            lax.fori_loop(0, KS, add, 0)

        def send_d(i):
            to_b, to_h, dev = ring_peer(i)
            pltpu.make_async_remote_copy(
                src_ref=ys.at[k, :, pl.ds(pl.multiple_of((to_b * 2 + to_h) * ZROWS, ZROWS), ZROWS), :],
                dst_ref=yr.at[k, ring],
                send_sem=dsend.at[k], recv_sem=drecv.at[k], device_id=dev, device_id_type=MESH,
            ).start()

        for i in range(1, 8):
            send_d(i)
        pltpu.make_async_copy(
            ys.at[k, :, pl.ds(pl.multiple_of(ring * ZROWS, ZROWS), ZROWS), :], yr.at[k, ring], drecv.at[k]
        ).start()
        pltpu.make_async_remote_copy(
            src_ref=es.at[k], dst_ref=er.at[k], send_sem=esend.at[k], recv_sem=erecv.at[k],
            device_id=ring_peer(4)[2], device_id_type=MESH,
        ).start()

    def stage_e(k):
        drain(yr.at[k], drecv.at[k])
        lz = tab["lz"][pl.ds(pl.multiple_of(ring * ZROWS, ZROWS), ZROWS), :]
        sign = twice(tab["sign"][0:ZROWS])
        for j in range(KS):
            a = decay(k, j, lz)
            g = a * a
            g = g * g
            g = g * g
            ends = [yr[k, 2 * b, j] + sign * yr[k, 2 * b + 1, j] for b in range(4)]
            total = ends[0]
            for b in range(1, 4):
                total = ends[b] + g * total
            g4 = g * g
            g4 = g4 * g4
            prev = total * (ALPHA / (1.0 - ALPHA * g4))
            for b in range(4):
                fs[k, b, j] = prev
                prev = ends[b] + g * prev

        def send_f(i):
            to_b, to_h, dev = ring_peer(i)
            pltpu.make_async_remote_copy(
                src_ref=fs.at[k, to_b],
                dst_ref=p.at[k, :, pl.ds(pl.multiple_of(ring * ZROWS, ZROWS), ZROWS), :],
                send_sem=fsend.at[k], recv_sem=frecv.at[k], device_id=dev, device_id_type=MESH,
            ).start()

        for i in range(1, 8):
            send_f(i)
        pltpu.make_async_copy(
            fs.at[k, block], p.at[k, :, pl.ds(pl.multiple_of(ring * ZROWS, ZROWS), ZROWS), :], frecv.at[k]
        ).start()

    def stage_g(k):
        drain(p.at[k], frecv.at[k])
        drain(er.at[k], erecv.at[k])
        mirrored = half.astype(F32)

        def one(j, c):
            a = decay(k, j, tab["lz"][...])
            ak = decay(k, j, tab["lk"][...])
            v = p[k, j] * twice(1.0 + mirrored * (tab["sign"][...] - 1.0))
            w = dot_left(tab["bz_i"][...], v)
            outer = [twice(tab["edges"][e]) for e in (2, 3)]
            walls = [twice(tab["walls"][e]) for e in range(2)]
            for t in range(BLOCK):
                v = v * a
                rhs = sq[k, t, j] + w
                for e in range(2):
                    row = jnp.sum(v * outer[e], axis=0, keepdims=True)
                    row = row + er[k, j, pl.ds(2 * t + e, 1), :] + ec[k, j, pl.ds(2 * t + e, 1), :]
                    rhs = rhs + walls[e] * row
                w = ak * rhs
                ws[k, t, j] = dot_left(tab["sine"][...], w)
            return c

        lax.fori_loop(0, KS, one, 0)

        def send_h(one):
            t, y, dev = plane_peer(one)
            pltpu.make_async_remote_copy(
                src_ref=ws.at[k, t, :, pl.ds(pl.multiple_of(y * PLANES, PLANES), PLANES), :],
                dst_ref=s2.at[pl.ds((k * PLACES + place) * KS, KS)],
                send_sem=hsend, recv_sem=hrecv.at[k], device_id=dev, device_id_type=MESH,
            ).start()

        for one in PEERS:
            send_h(one)
        pltpu.make_async_copy(
            ws.at[k, step, :, pl.ds(pl.multiple_of(slab * PLANES, PLANES), PLANES), :],
            s2.at[pl.ds((k * PLACES + place) * KS, KS)],
            hrecv.at[k],
        ).start()

    for k in range(SETS):
        stage_c(k)
        if k > 0:
            stage_e(k - 1)
        if k > 1:
            stage_g(k - 2)
    stage_e(SETS - 1)
    stage_g(SETS - 2)
    stage_g(SETS - 1)

    for k in range(SETS):
        rows = pl.ds(k * PLACES * KS, PLACES * KS)
        drain(s2.at[rows], hrecv.at[k])
        back = dot_right(s2[rows].reshape(PLACES * KS * PLANES, NX), tab["bx_i"][...])
        ty[rows] = back.reshape(PLACES * KS, PLANES, NX)

    @pl.when(last)
    def _():
        drain(u, rsend)

    def store(g):
        return pltpu.make_async_copy(u.at[pl.ds(4 * g, 4)], out_ref.at[0, pl.ds(4 * g, 4)], osem.at[g])

    for g in range(PLANES // 4):
        for i in range(4):
            u[4 * g + i] = dot_left(tab["by_i"][...], ty[:, 4 * g + i, :])
        store(g).start()

    for k in range(SETS):
        drain(s.at[pl.ds(0, 31 * KS)], bsend.at[k])
        drain(p.at[k, :, pl.ds(0, 7 * ZROWS), :], dsend.at[k])
        drain(es.at[k], esend.at[k])
        drain(p.at[k, :, pl.ds(0, 7 * ZROWS), :], fsend.at[k])
    drain(s2.at[pl.ds(0, 31 * ROWS)], hsend)

    @pl.when(helper)
    def _():
        drain(sp.at[pl.ds(0, PLACES - 1)], psend)

    @pl.when(above)
    def _():
        drain(sp.at[0], psend)

    for g in range(PLANES // 4):
        store(g).wait()


def body(iterate, initial):
    dma = pltpu.SemaphoreType.DMA
    vmem = pl.BlockSpec(memory_space=pltpu.VMEM)
    hbm = pl.BlockSpec(memory_space=pl.ANY)
    return pl.pallas_call(
        kernel,
        out_shape=jax.ShapeDtypeStruct(iterate.shape, F32),
        in_specs=[hbm, hbm] + [vmem] * len(NAMES),
        out_specs=hbm,
        scratch_shapes=[
            pltpu.VMEM((PLANES, NY, NX), F32),
            pltpu.VMEM((NY, PLANES, NX), F32),
            pltpu.VMEM((NY, PLANES, NX), F32),
            pltpu.VMEM((HELP, NY, NX), F32),
            pltpu.VMEM((HELP, NY, NX), F32),
            pltpu.VMEM((PLACES, HELP * ROWS, NX), F32),
            pltpu.VMEM((SETS, BLOCK, KS, HALF, NX), F32),
            pltpu.VMEM((PLACES, HELP * ROWS, NX), F32),
            pltpu.VMEM((SETS, BLOCK, KS, HALF, NX), F32),
            pltpu.VMEM((SETS, KS, NZ, NX), F32),
            pltpu.VMEM((SETS, 8, KS, ZROWS, NX), F32),
            pltpu.VMEM((SETS, KS, 2 * BLOCK, NX), F32),
            pltpu.VMEM((SETS, KS, 2 * BLOCK, NX), F32),
            pltpu.VMEM((SETS, KS, 2 * BLOCK, NX), F32),
            pltpu.VMEM((SETS, 4, KS, ZROWS, NX), F32),
            pltpu.VMEM((SETS, KS, NZ, NX), F32),
            pltpu.VMEM((SETS, BLOCK, KS, HALF, NX), F32),
            pltpu.VMEM((NY, PLANES, NX), F32),
            dma, dma, dma((PLANES // 4,)),
            dma((SETS,)), dma((SETS,)), dma, dma, dma, dma,
            dma((SETS,)), dma((SETS,)), dma((SETS,)), dma((SETS,)), dma((SETS,)), dma((SETS,)),
            dma, dma((SETS,)),
        ],
        compiler_params=pltpu.CompilerParams(
            collective_id=0, has_side_effects=True, vmem_limit_bytes=56 * 1024 * 1024
        ),
        cost_estimate=pl.CostEstimate(flops=4 * 10**9, bytes_accessed=6 * 2**20, transcendentals=0),
        name="paradiag",
    )(iterate, initial, *[jnp.asarray(TABLES[n]) for n in NAMES])


def solution(mesh):
    return jax.shard_map(
        body,
        mesh=mesh,
        in_specs=(P("tm", "gz", None, None), P("gz", None, None)),
        out_specs=P("tm", "gz", None, None),
        check_vma=False,
    )
```

```python
import functools
import math

import jax
import jax.numpy as jnp
import ml_dtypes
import numpy as np
from jax import lax
from jax.experimental import pallas as pl
from jax.experimental.pallas import tpu as pltpu
from jax.sharding import PartitionSpec as P

MESH = pl.DeviceIdType.MESH
F32 = jnp.float32
BF16 = jnp.bfloat16

NX, NY, NZ, L = 256, 128, 128, 32
TIME_STEP, DIFFUSION, ALPHA, STABILIZER = 0.05, 200.0, 0.05, 2.0
COUPLING = TIME_STEP * DIFFUSION
BLOCK = 8
SLABS = 4
HALF = NZ // 2
PLANES = 16
ROWS = 4
PLACES = 32
HELP = 2
HELP_AFTER = 0
SETS = 4
KS = ROWS // SETS
ZROWS = 16


def peers():
    found = []
    every = [(x, core, y) for x in range(4) for core in range(2) for y in range(SLABS)]
    every.sort(key=lambda one: -min(one[0], 4 - one[0]) - min(one[2], 4 - one[2]))
    for x, core, y in every:
        for one in ((x, core, y), (y, core, x), (-x % 4, core, -y % 4), (-y % 4, core, -x % 4)):
            if one not in found and one != (0, 0, 0):
                found.append(one)
    return found


PEERS = peers()


def real_basis(n):
    pos = np.arange(n)
    rows, freq = [np.ones(n) / math.sqrt(n), np.cos(math.pi * pos) / math.sqrt(n)], [0, n // 2]
    for m in range(1, n // 2):
        rows += [np.cos(2 * math.pi * m * pos / n) * math.sqrt(2 / n)]
        rows += [np.sin(2 * math.pi * m * pos / n) * math.sqrt(2 / n)]
        freq += [m, m]
    return np.stack(rows), 2.0 - 2.0 * np.cos(2 * math.pi * np.array(freq) / n)


def parts(m):
    m = np.asarray(m, np.float32)
    hi = m.astype(ml_dtypes.bfloat16)
    return hi, (m - hi.astype(np.float32)).astype(ml_dtypes.bfloat16)


def left(m):
    hi, lo = parts(m)
    return np.concatenate([hi, lo, hi], axis=1)


def right(m):
    hi, lo = parts(m)
    return np.concatenate([hi, lo, hi], axis=0)


def wide(column):
    return np.broadcast_to(np.asarray(column, np.float32)[:, None], (len(column), 128)).copy()


def tables():
    bx, lx = real_basis(NX)
    by, ly = real_basis(NY)
    bz, lz = real_basis(NZ)
    k = np.arange(1, HALF + 1)
    sine = np.sin(math.pi * np.outer(k, k) / (HALF + 1)) * math.sqrt(2 / (HALF + 1))
    lk = 2.0 - 2.0 * np.cos(math.pi * k / (HALF + 1))
    sign = np.where((np.arange(NZ) // 2) % 2 == 0, 1.0, -1.0)
    base = 1.0 + TIME_STEP * STABILIZER
    return dict(
        bx_f=right(bx.T),
        by_f=left(by),
        bx_i=right(bx),
        by_i=left(by.T),
        bz_s=left(np.concatenate([bz[:, :HALF], sine], axis=0)),
        bz_p=left(bz[:, [i + HELP * n for i in range(HELP) for n in range(HALF // HELP)]]),
        bz_i=left(sine @ bz[:, :HALF].T),
        sine=left(sine),
        lxy=(base + COUPLING * (ly[:, None] + lx[None, :])).astype(np.float32),
        lz=wide(COUPLING * lz),
        lk=wide(COUPLING * lk),
        sign=wide(sign),
        edges=np.stack([wide(bz[:, p]) for p in (HALF - 1, 0, NZ - 1, HALF)]),
        walls=np.stack([wide(COUPLING * sine[:, 0]), wide(COUPLING * sine[:, HALF - 1])]),
    )


TABLES = tables()
NAMES = sorted(TABLES)


def split(x):
    hi = x.astype(BF16)
    return hi, (x - hi.astype(F32)).astype(BF16)


def dot(a, b):
    return jnp.dot(a, b, preferred_element_type=F32)


def dot_left(table, x):
    hi, lo = split(x)
    return dot(table, jnp.concatenate([hi, hi, lo], axis=0))


def dot_right(x, table):
    hi, lo = split(x)
    return dot(jnp.concatenate([hi, hi, lo], axis=1), table)


def twice(x):
    return jnp.concatenate([x, x], axis=1)


def drain(ref, sem):
    pltpu.make_async_copy(ref, ref, sem).wait()


def kernel(u_ref, init_ref, *refs):
    tab = dict(zip(NAMES, refs[: len(NAMES)]))
    (out_ref, u, ty, s, pa, hp, sp, r, pb, sq, ys, yr, es, ec, er, fs, p, ws, s2,
     usem, isem, osem, bsend, brecv, rsend, rrecv, psend, precv,
     dsend, drecv, esend, erecv, fsend, frecv, hsend, hrecv) = refs[len(NAMES):]
    tm, gz = lax.axis_index("tm"), lax.axis_index("gz")
    block, step = tm // BLOCK, tm % BLOCK
    half, slab = gz // SLABS, gz % SLABS
    place = step * SLABS + slab
    ring = block * 2 + half
    x, core = step // 2, step % 2
    last = tm == L - 1
    beside = jnp.logical_and(block == 3, jnp.logical_or(x % 2 == 0, step == BLOCK - 2))
    above = jnp.logical_and(x == 3, jnp.logical_or(block == 2, jnp.logical_and(block == 1, core == 0)))
    helper = jnp.logical_or(beside, above)
    part = jnp.where(block == 3, jnp.where(x == 3, 4, x + core), jnp.where(block == 2, 5 + core, 7))

    load = pltpu.make_async_copy(u_ref.at[0], u, usem)
    load.start()

    state = pltpu.make_async_copy(init_ref.at[pl.ds(part * HELP, HELP)], pa, isem)

    @pl.when(helper)
    def _():
        state.start()

    def plane_peer(one):
        dx, dc, dy = one
        t, y = (x + dx) % 4 * 2 + (core + dc) % 2, (slab + dy) % SLABS
        return t, y, (block * BLOCK + t, half * SLABS + y)

    def ring_peer(i):
        to_b, to_h = (block + i % 4) % 4, (half + i // 4) % 2
        return to_b, to_h, (to_b * BLOCK + step, to_h * SLABS + slab)

    barrier = pltpu.get_barrier_semaphore()

    def greet(dev):
        pl.semaphore_signal(barrier, inc=1, device_id=dev, device_id_type=MESH)

    for one in PEERS:
        greet(plane_peer(one)[2])
    for i in range(1, 8):
        greet(ring_peer(i)[2])

    @pl.when(block == 3)
    def _():
        for y in range(SLABS):
            for c in range(2):
                greet((2 * BLOCK + 6 + c, half * SLABS + y))
            greet((BLOCK + 6, half * SLABS + y))

    @pl.when(jnp.logical_and(above, core == 0))
    def _():
        greet((L - 1, gz))

    greeted = PLACES - 1 + 7

    @pl.when(last)
    def _():
        pl.semaphore_wait(barrier, greeted + 2)

    load.wait()

    @pl.when(last)
    def _():
        for c in range(4 * HELP):
            for q in (0, 2, 5, 4, 1, 3, 6, 7):
                where = (pl.ds(c // 4, 1), pl.ds(c % 4 * 32, 32))
                pltpu.make_async_remote_copy(
                    src_ref=u.at[pl.ds(q * HELP + c // 4, 1), where[1]], dst_ref=hp.at[where],
                    send_sem=rsend, recv_sem=rrecv,
                    device_id=((24, 25, 28, 29, 30, 22, 23, 14)[q], gz), device_id_type=MESH,
                ).start()


    def along_y(x, dst, z):
        for i in range(4):
            dst[:, z + i, :] = dot_left(tab["by_f"][...], x[i])

    def along_x(k):
        rows = pl.ds(k * PLACES * KS, PLACES * KS)
        done = dot_right(ty[rows].reshape(PLACES * KS * PLANES, NX), tab["bx_f"][...])
        s[rows] = done.reshape(PLACES * KS, PLANES, NX)

    for g in range(PLANES // 4):
        v = u[4 * g:4 * g + 4]
        along_y(v * (TIME_STEP * (STABILIZER + 1.0) - TIME_STEP * v * v), ty, 4 * g)

    @pl.when(above)
    def _():
        pl.semaphore_wait(barrier, greeted + PLACES)

    @pl.when(jnp.logical_not(jnp.logical_or(above, last)))
    def _():
        pl.semaphore_wait(barrier, greeted)

    def send_b(one, k):
        t, y, dev = plane_peer(one)
        pltpu.make_async_remote_copy(
            src_ref=s.at[pl.ds((k * PLACES + t * SLABS + y) * KS, KS)],
            dst_ref=r.at[k, step, :, pl.ds(pl.multiple_of(slab * PLANES, PLANES), PLANES), :],
            send_sem=bsend.at[k], recv_sem=brecv.at[k], device_id=dev, device_id_type=MESH,
        ).start()

    def send_p(one):
        t, y, _ = plane_peer(one)
        pltpu.make_async_remote_copy(
            src_ref=sp.at[t * SLABS + y], dst_ref=pb.at[slab * 8 + part],
            send_sem=psend, recv_sem=precv, device_id=(3 * BLOCK + t, half * SLABS + y), device_id_type=MESH,
        ).start()

    for k in range(SETS):
        along_x(k)
        for one in PEERS:
            send_b(one, k)
        pltpu.make_async_copy(
            s.at[pl.ds((k * PLACES + place) * KS, KS)],
            r.at[k, step, :, pl.ds(pl.multiple_of(slab * PLANES, PLANES), PLANES), :],
            brecv.at[k],
        ).start()
        if k != HELP_AFTER:
            continue


        @pl.when(helper)
        def _():
            state.wait()
            drain(hp, rrecv)
            rows = [dot_left(tab["by_f"][...], pa[i] * (1.0 / ALPHA) - hp[i]) for i in range(HELP)]
            rows = dot_right(jnp.concatenate(rows, axis=0), tab["bx_f"][...])
            for i in range(HELP):
                for m in range(ROWS):
                    sp[:, HELP * m + i, :] = rows[i * NY + m * PLACES:i * NY + (m + 1) * PLACES]
            for one in PEERS:
                send_p(one)

        @pl.when(beside)
        def _():
            pltpu.make_async_copy(sp.at[place], pb.at[slab * 8 + part], precv).start()

        @pl.when(above)
        def _():
            send_p((0, 0, 0))

    def decay(k, j, table):
        row = tab["lxy"][pl.ds((k * PLACES + place) * KS + j, 1), :]
        return 1.0 / (row + twice(table))

    def stage_c(k):
        drain(r.at[k], brecv.at[k])

        if k == 0:
            @pl.when(block == 3)
            def _():
                drain(pb, precv)

        def one(j, c):
            a = decay(k, j, tab["lz"][...])
            z = None
            edges = [twice(tab["edges"][e]) for e in range(4)]
            for t in range(BLOCK):
                both = dot_left(tab["bz_s"][...], r[k, t, j])
                sq[k, t, j] = both[NZ:]
                z = a * both[:NZ] if z is None else a * (both[:NZ] + z)
                for e in range(4):
                    row = jnp.sum(z * edges[e], axis=0, keepdims=True)
                    if e < 2:
                        es[k, j, pl.ds(2 * t + e, 1), :] = row
                    else:
                        ec[k, j, pl.ds(2 * t + e - 2, 1), :] = row
            ys[k, j] = z
            return c

        lax.fori_loop(0, KS, one, 0)

        @pl.when(block == 3)
        def _():
            def add(j, c):
                extra = [pb[:, HELP * k + i, :] for i in range(HELP)]
                ys[k, j] += dot_left(tab["bz_p"][...], jnp.concatenate(extra, axis=0))
                return c
            lax.fori_loop(0, KS, add, 0)

        def send_d(i):
            to_b, to_h, dev = ring_peer(i)
            pltpu.make_async_remote_copy(
                src_ref=ys.at[k, :, pl.ds(pl.multiple_of((to_b * 2 + to_h) * ZROWS, ZROWS), ZROWS), :],
                dst_ref=yr.at[k, ring],
                send_sem=dsend.at[k], recv_sem=drecv.at[k], device_id=dev, device_id_type=MESH,
            ).start()

        for i in range(1, 8):
            send_d(i)
        pltpu.make_async_copy(
            ys.at[k, :, pl.ds(pl.multiple_of(ring * ZROWS, ZROWS), ZROWS), :], yr.at[k, ring], drecv.at[k]
        ).start()
        pltpu.make_async_remote_copy(
            src_ref=es.at[k], dst_ref=er.at[k], send_sem=esend.at[k], recv_sem=erecv.at[k],
            device_id=ring_peer(4)[2], device_id_type=MESH,
        ).start()

    def stage_e(k):
        drain(yr.at[k], drecv.at[k])
        lz = tab["lz"][pl.ds(pl.multiple_of(ring * ZROWS, ZROWS), ZROWS), :]
        sign = twice(tab["sign"][0:ZROWS])
        for j in range(KS):
            a = decay(k, j, lz)
            g = a * a
            g = g * g
            g = g * g
            ends = [yr[k, 2 * b, j] + sign * yr[k, 2 * b + 1, j] for b in range(4)]
            total = ends[0]
            for b in range(1, 4):
                total = ends[b] + g * total
            g4 = g * g
            g4 = g4 * g4
            prev = total * (ALPHA / (1.0 - ALPHA * g4))
            for b in range(4):
                fs[k, b, j] = prev
                prev = ends[b] + g * prev

        def send_f(i):
            to_b, to_h, dev = ring_peer(i)
            pltpu.make_async_remote_copy(
                src_ref=fs.at[k, to_b],
                dst_ref=p.at[k, :, pl.ds(pl.multiple_of(ring * ZROWS, ZROWS), ZROWS), :],
                send_sem=fsend.at[k], recv_sem=frecv.at[k], device_id=dev, device_id_type=MESH,
            ).start()

        for i in range(1, 8):
            send_f(i)
        pltpu.make_async_copy(
            fs.at[k, block], p.at[k, :, pl.ds(pl.multiple_of(ring * ZROWS, ZROWS), ZROWS), :], frecv.at[k]
        ).start()

    def stage_g(k):
        drain(p.at[k], frecv.at[k])
        drain(er.at[k], erecv.at[k])
        mirrored = half.astype(F32)

        def one(j, c):
            a = decay(k, j, tab["lz"][...])
            ak = decay(k, j, tab["lk"][...])
            v = p[k, j] * twice(1.0 + mirrored * (tab["sign"][...] - 1.0))
            w = dot_left(tab["bz_i"][...], v)
            outer = [twice(tab["edges"][e]) for e in (2, 3)]
            walls = [twice(tab["walls"][e]) for e in range(2)]
            for t in range(BLOCK):
                v = v * a
                rhs = sq[k, t, j] + w
                for e in range(2):
                    row = jnp.sum(v * outer[e], axis=0, keepdims=True)
                    row = row + er[k, j, pl.ds(2 * t + e, 1), :] + ec[k, j, pl.ds(2 * t + e, 1), :]
                    rhs = rhs + walls[e] * row
                w = ak * rhs
                ws[k, t, j] = dot_left(tab["sine"][...], w)
            return c

        lax.fori_loop(0, KS, one, 0)

        def send_h(one):
            t, y, dev = plane_peer(one)
            pltpu.make_async_remote_copy(
                src_ref=ws.at[k, t, :, pl.ds(pl.multiple_of(y * PLANES, PLANES), PLANES), :],
                dst_ref=s2.at[pl.ds((k * PLACES + place) * KS, KS)],
                send_sem=hsend, recv_sem=hrecv.at[k], device_id=dev, device_id_type=MESH,
            ).start()

        for one in PEERS:
            send_h(one)
        pltpu.make_async_copy(
            ws.at[k, step, :, pl.ds(pl.multiple_of(slab * PLANES, PLANES), PLANES), :],
            s2.at[pl.ds((k * PLACES + place) * KS, KS)],
            hrecv.at[k],
        ).start()

    for k in range(SETS):
        stage_c(k)
        if k > 0:
            stage_e(k - 1)
        if k > 1:
            stage_g(k - 2)
    stage_e(SETS - 1)
    stage_g(SETS - 2)
    stage_g(SETS - 1)

    for k in range(SETS):
        rows = pl.ds(k * PLACES * KS, PLACES * KS)
        drain(s2.at[rows], hrecv.at[k])
        back = dot_right(s2[rows].reshape(PLACES * KS * PLANES, NX), tab["bx_i"][...])
        ty[rows] = back.reshape(PLACES * KS, PLANES, NX)

    @pl.when(last)
    def _():
        drain(u, rsend)

    def store(g):
        return pltpu.make_async_copy(u.at[pl.ds(4 * g, 4)], out_ref.at[0, pl.ds(4 * g, 4)], osem.at[g])

    for g in range(PLANES // 4):
        for i in range(4):
            u[4 * g + i] = dot_left(tab["by_i"][...], ty[:, 4 * g + i, :])
        store(g).start()

    for k in range(SETS):
        drain(s.at[pl.ds(0, 31 * KS)], bsend.at[k])
        drain(p.at[k, :, pl.ds(0, 7 * ZROWS), :], dsend.at[k])
        drain(es.at[k], esend.at[k])
        drain(p.at[k, :, pl.ds(0, 7 * ZROWS), :], fsend.at[k])
    drain(s2.at[pl.ds(0, 31 * ROWS)], hsend)

    @pl.when(helper)
    def _():
        drain(sp.at[pl.ds(0, PLACES - 1)], psend)

    @pl.when(above)
    def _():
        drain(sp.at[0], psend)

    for g in range(PLANES // 4):
        store(g).wait()


def body(iterate, initial):
    dma = pltpu.SemaphoreType.DMA
    vmem = pl.BlockSpec(memory_space=pltpu.VMEM)
    hbm = pl.BlockSpec(memory_space=pl.ANY)
    return pl.pallas_call(
        kernel,
        out_shape=jax.ShapeDtypeStruct(iterate.shape, F32),
        in_specs=[hbm, hbm] + [vmem] * len(NAMES),
        out_specs=hbm,
        scratch_shapes=[
            pltpu.VMEM((PLANES, NY, NX), F32),
            pltpu.VMEM((NY, PLANES, NX), F32),
            pltpu.VMEM((NY, PLANES, NX), F32),
            pltpu.VMEM((HELP, NY, NX), F32),
            pltpu.VMEM((HELP, NY, NX), F32),
            pltpu.VMEM((PLACES, HELP * ROWS, NX), F32),
            pltpu.VMEM((SETS, BLOCK, KS, HALF, NX), F32),
            pltpu.VMEM((PLACES, HELP * ROWS, NX), F32),
            pltpu.VMEM((SETS, BLOCK, KS, HALF, NX), F32),
            pltpu.VMEM((SETS, KS, NZ, NX), F32),
            pltpu.VMEM((SETS, 8, KS, ZROWS, NX), F32),
            pltpu.VMEM((SETS, KS, 2 * BLOCK, NX), F32),
            pltpu.VMEM((SETS, KS, 2 * BLOCK, NX), F32),
            pltpu.VMEM((SETS, KS, 2 * BLOCK, NX), F32),
            pltpu.VMEM((SETS, 4, KS, ZROWS, NX), F32),
            pltpu.VMEM((SETS, KS, NZ, NX), F32),
            pltpu.VMEM((SETS, BLOCK, KS, HALF, NX), F32),
            pltpu.VMEM((NY, PLANES, NX), F32),
            dma, dma, dma((PLANES // 4,)),
            dma((SETS,)), dma((SETS,)), dma, dma, dma, dma,
            dma((SETS,)), dma((SETS,)), dma((SETS,)), dma((SETS,)), dma((SETS,)), dma((SETS,)),
            dma, dma((SETS,)),
        ],
        compiler_params=pltpu.CompilerParams(
            collective_id=0, has_side_effects=True, vmem_limit_bytes=56 * 1024 * 1024
        ),
        cost_estimate=pl.CostEstimate(flops=4 * 10**9, bytes_accessed=6 * 2**20, transcendentals=0),
        name="paradiag",
    )(iterate, initial, *[jnp.asarray(TABLES[n]) for n in NAMES])


def solution(mesh):
    return jax.shard_map(
        body,
        mesh=mesh,
        in_specs=(P("tm", "gz", None, None), P("gz", None, None)),
        out_specs=P("tm", "gz", None, None),
        check_vma=False,
    )
```

```python
import functools
import math

import jax
import jax.numpy as jnp
import ml_dtypes
import numpy as np
from jax import lax
from jax.experimental import pallas as pl
from jax.experimental.pallas import tpu as pltpu
from jax.sharding import PartitionSpec as P

MESH = pl.DeviceIdType.MESH
F32 = jnp.float32
BF16 = jnp.bfloat16

NX, NY, NZ, L = 256, 128, 128, 32
TIME_STEP, DIFFUSION, ALPHA, STABILIZER = 0.05, 200.0, 0.05, 2.0
COUPLING = TIME_STEP * DIFFUSION
BLOCK = 8
SLABS = 4
HALF = NZ // 2
PLANES = 16
ROWS = 4
PLACES = 32
HELP = 2
HELP_AFTER = 0
SETS = 4
KS = ROWS // SETS
ZROWS = 16


def peers():
    found = []
    for x in range(4):
        for core in range(2):
            for y in range(SLABS):
                for one in ((x, core, y), (-x % 4, core, -y % SLABS)):
                    if one not in found and one != (0, 0, 0):
                        found.append(one)
    return found


PEERS = peers()


def real_basis(n):
    pos = np.arange(n)
    rows, freq = [np.ones(n) / math.sqrt(n), np.cos(math.pi * pos) / math.sqrt(n)], [0, n // 2]
    for m in range(1, n // 2):
        rows += [np.cos(2 * math.pi * m * pos / n) * math.sqrt(2 / n)]
        rows += [np.sin(2 * math.pi * m * pos / n) * math.sqrt(2 / n)]
        freq += [m, m]
    return np.stack(rows), 2.0 - 2.0 * np.cos(2 * math.pi * np.array(freq) / n)


def parts(m):
    m = np.asarray(m, np.float32)
    hi = m.astype(ml_dtypes.bfloat16)
    return hi, (m - hi.astype(np.float32)).astype(ml_dtypes.bfloat16)


def left(m):
    hi, lo = parts(m)
    return np.concatenate([hi, lo, hi], axis=1)


def right(m):
    hi, lo = parts(m)
    return np.concatenate([hi, lo, hi], axis=0)


def wide(column):
    return np.broadcast_to(np.asarray(column, np.float32)[:, None], (len(column), 128)).copy()


def tables():
    bx, lx = real_basis(NX)
    by, ly = real_basis(NY)
    bz, lz = real_basis(NZ)
    k = np.arange(1, HALF + 1)
    sine = np.sin(math.pi * np.outer(k, k) / (HALF + 1)) * math.sqrt(2 / (HALF + 1))
    lk = 2.0 - 2.0 * np.cos(math.pi * k / (HALF + 1))
    sign = np.where((np.arange(NZ) // 2) % 2 == 0, 1.0, -1.0)
    base = 1.0 + TIME_STEP * STABILIZER
    return dict(
        bx_f=right(bx.T),
        by_f=left(by),
        bx_i=right(bx),
        by_i=left(by.T),
        bz_s=left(np.concatenate([bz[:, :HALF], sine], axis=0)),
        bz_p=left(bz[:, [i + HELP * n for i in range(HELP) for n in range(HALF // HELP)]]),
        bz_i=left(sine @ bz[:, :HALF].T),
        sine=left(sine),
        lxy=(base + COUPLING * (ly[:, None] + lx[None, :])).astype(np.float32),
        lz=wide(COUPLING * lz),
        lk=wide(COUPLING * lk),
        sign=wide(sign),
        edges=np.stack([wide(bz[:, p]) for p in (HALF - 1, 0, NZ - 1, HALF)]),
        walls=np.stack([wide(COUPLING * sine[:, 0]), wide(COUPLING * sine[:, HALF - 1])]),
    )


TABLES = tables()
NAMES = sorted(TABLES)


def split(x):
    hi = x.astype(BF16)
    return hi, (x - hi.astype(F32)).astype(BF16)


def dot(a, b):
    return jnp.dot(a, b, preferred_element_type=F32)


def dot_left(table, x):
    hi, lo = split(x)
    return dot(table, jnp.concatenate([hi, hi, lo], axis=0))


def dot_right(x, table):
    hi, lo = split(x)
    return dot(jnp.concatenate([hi, hi, lo], axis=1), table)


def twice(x):
    return jnp.concatenate([x, x], axis=1)


def drain(ref, sem):
    pltpu.make_async_copy(ref, ref, sem).wait()


def kernel(u_ref, init_ref, *refs):
    tab = dict(zip(NAMES, refs[: len(NAMES)]))
    (out_ref, u, ty, s, pa, hp, sp, r, pb, sq, ys, yr, es, ec, er, fs, p, ws, s2,
     usem, isem, osem, bsend, brecv, rsend, rrecv, psend, precv,
     dsend, drecv, esend, erecv, fsend, frecv, hsend, hrecv) = refs[len(NAMES):]
    tm, gz = lax.axis_index("tm"), lax.axis_index("gz")
    block, step = tm // BLOCK, tm % BLOCK
    half, slab = gz // SLABS, gz % SLABS
    place = step * SLABS + slab
    ring = block * 2 + half
    x, core = step // 2, step % 2
    last = tm == L - 1
    beside = jnp.logical_and(block == 3, jnp.logical_or(x % 2 == 0, step == BLOCK - 2))
    above = jnp.logical_and(x == 3, jnp.logical_or(block == 2, jnp.logical_and(block == 1, core == 0)))
    helper = jnp.logical_or(beside, above)
    part = jnp.where(block == 3, jnp.where(x == 3, 4, x + core), jnp.where(block == 2, 5 + core, 7))

    load = pltpu.make_async_copy(u_ref.at[0], u, usem)
    load.start()

    state = pltpu.make_async_copy(init_ref.at[pl.ds(part * HELP, HELP)], pa, isem)

    @pl.when(helper)
    def _():
        state.start()

    def plane_peer(one):
        dx, dc, dy = one
        t, y = (x + dx) % 4 * 2 + (core + dc) % 2, (slab + dy) % SLABS
        return t, y, (block * BLOCK + t, half * SLABS + y)

    def ring_peer(i):
        to_b, to_h = (block + i % 4) % 4, (half + i // 4) % 2
        return to_b, to_h, (to_b * BLOCK + step, to_h * SLABS + slab)

    barrier = pltpu.get_barrier_semaphore()

    def greet(dev):
        pl.semaphore_signal(barrier, inc=1, device_id=dev, device_id_type=MESH)

    for one in PEERS:
        greet(plane_peer(one)[2])
    for i in range(1, 8):
        greet(ring_peer(i)[2])

    @pl.when(block == 3)
    def _():
        for y in range(SLABS):
            for c in range(2):
                greet((2 * BLOCK + 6 + c, half * SLABS + y))
            greet((BLOCK + 6, half * SLABS + y))

    @pl.when(jnp.logical_and(above, core == 0))
    def _():
        greet((L - 1, gz))

    greeted = PLACES - 1 + 7

    @pl.when(last)
    def _():
        pl.semaphore_wait(barrier, greeted + 2)

    load.wait()

    @pl.when(last)
    def _():
        for c in range(4 * HELP):
            for q in (5, 0, 2, 6, 1, 3, 7, 4):
                where = (pl.ds(c // 4, 1), pl.ds(c % 4 * 32, 32))
                pltpu.make_async_remote_copy(
                    src_ref=u.at[pl.ds(q * HELP + c // 4, 1), where[1]], dst_ref=hp.at[where],
                    send_sem=rsend, recv_sem=rrecv,
                    device_id=((24, 25, 28, 29, 30, 22, 23, 14)[q], gz), device_id_type=MESH,
                ).start()


    def along_y(x, dst, z):
        for i in range(4):
            dst[:, z + i, :] = dot_left(tab["by_f"][...], x[i])

    def along_x(k):
        rows = pl.ds(k * PLACES * KS, PLACES * KS)
        done = dot_right(ty[rows].reshape(PLACES * KS * PLANES, NX), tab["bx_f"][...])
        s[rows] = done.reshape(PLACES * KS, PLANES, NX)

    for g in range(PLANES // 4):
        v = u[4 * g:4 * g + 4]
        along_y(v * (TIME_STEP * (STABILIZER + 1.0) - TIME_STEP * v * v), ty, 4 * g)

    @pl.when(above)
    def _():
        pl.semaphore_wait(barrier, greeted + PLACES)

    @pl.when(jnp.logical_not(jnp.logical_or(above, last)))
    def _():
        pl.semaphore_wait(barrier, greeted)

    def send_b(one, k):
        t, y, dev = plane_peer(one)
        pltpu.make_async_remote_copy(
            src_ref=s.at[pl.ds((k * PLACES + t * SLABS + y) * KS, KS)],
            dst_ref=r.at[k, step, :, pl.ds(pl.multiple_of(slab * PLANES, PLANES), PLANES), :],
            send_sem=bsend.at[k], recv_sem=brecv.at[k], device_id=dev, device_id_type=MESH,
        ).start()

    def send_p(one):
        t, y, _ = plane_peer(one)
        pltpu.make_async_remote_copy(
            src_ref=sp.at[t * SLABS + y], dst_ref=pb.at[slab * 8 + part],
            send_sem=psend, recv_sem=precv, device_id=(3 * BLOCK + t, half * SLABS + y), device_id_type=MESH,
        ).start()

    for k in range(SETS):
        along_x(k)
        for one in PEERS:
            send_b(one, k)
        pltpu.make_async_copy(
            s.at[pl.ds((k * PLACES + place) * KS, KS)],
            r.at[k, step, :, pl.ds(pl.multiple_of(slab * PLANES, PLANES), PLANES), :],
            brecv.at[k],
        ).start()
        if k != HELP_AFTER:
            continue


        @pl.when(helper)
        def _():
            state.wait()
            drain(hp, rrecv)
            rows = [dot_left(tab["by_f"][...], pa[i] * (1.0 / ALPHA) - hp[i]) for i in range(HELP)]
            rows = dot_right(jnp.concatenate(rows, axis=0), tab["bx_f"][...])
            for i in range(HELP):
                for m in range(ROWS):
                    sp[:, HELP * m + i, :] = rows[i * NY + m * PLACES:i * NY + (m + 1) * PLACES]
            for one in PEERS:
                send_p(one)

        @pl.when(beside)
        def _():
            pltpu.make_async_copy(sp.at[place], pb.at[slab * 8 + part], precv).start()

        @pl.when(above)
        def _():
            send_p((0, 0, 0))

    def decay(k, j, table):
        row = tab["lxy"][pl.ds((k * PLACES + place) * KS + j, 1), :]
        return 1.0 / (row + twice(table))

    def stage_c(k):
        drain(r.at[k], brecv.at[k])

        if k == 0:
            @pl.when(block == 3)
            def _():
                drain(pb, precv)

        def one(j, c):
            a = decay(k, j, tab["lz"][...])
            z = None
            edges = [twice(tab["edges"][e]) for e in range(4)]
            for t in range(BLOCK):
                both = dot_left(tab["bz_s"][...], r[k, t, j])
                sq[k, t, j] = both[NZ:]
                z = a * both[:NZ] if z is None else a * (both[:NZ] + z)
                for e in range(4):
                    row = jnp.sum(z * edges[e], axis=0, keepdims=True)
                    if e < 2:
                        es[k, j, pl.ds(2 * t + e, 1), :] = row
                    else:
                        ec[k, j, pl.ds(2 * t + e - 2, 1), :] = row
            ys[k, j] = z
            return c

        lax.fori_loop(0, KS, one, 0)

        @pl.when(block == 3)
        def _():
            def add(j, c):
                extra = [pb[:, HELP * k + i, :] for i in range(HELP)]
                ys[k, j] += dot_left(tab["bz_p"][...], jnp.concatenate(extra, axis=0))
                return c
            lax.fori_loop(0, KS, add, 0)

        def send_d(i):
            to_b, to_h, dev = ring_peer(i)
            pltpu.make_async_remote_copy(
                src_ref=ys.at[k, :, pl.ds(pl.multiple_of((to_b * 2 + to_h) * ZROWS, ZROWS), ZROWS), :],
                dst_ref=yr.at[k, ring],
                send_sem=dsend.at[k], recv_sem=drecv.at[k], device_id=dev, device_id_type=MESH,
            ).start()

        for i in range(1, 8):
            send_d(i)
        pltpu.make_async_copy(
            ys.at[k, :, pl.ds(pl.multiple_of(ring * ZROWS, ZROWS), ZROWS), :], yr.at[k, ring], drecv.at[k]
        ).start()
        pltpu.make_async_remote_copy(
            src_ref=es.at[k], dst_ref=er.at[k], send_sem=esend.at[k], recv_sem=erecv.at[k],
            device_id=ring_peer(4)[2], device_id_type=MESH,
        ).start()

    def stage_e(k):
        drain(yr.at[k], drecv.at[k])
        lz = tab["lz"][pl.ds(pl.multiple_of(ring * ZROWS, ZROWS), ZROWS), :]
        sign = twice(tab["sign"][0:ZROWS])
        for j in range(KS):
            a = decay(k, j, lz)
            g = a * a
            g = g * g
            g = g * g
            ends = [yr[k, 2 * b, j] + sign * yr[k, 2 * b + 1, j] for b in range(4)]
            total = ends[0]
            for b in range(1, 4):
                total = ends[b] + g * total
            g4 = g * g
            g4 = g4 * g4
            prev = total * (ALPHA / (1.0 - ALPHA * g4))
            for b in range(4):
                fs[k, b, j] = prev
                prev = ends[b] + g * prev

        def send_f(i):
            to_b, to_h, dev = ring_peer(i)
            pltpu.make_async_remote_copy(
                src_ref=fs.at[k, to_b],
                dst_ref=p.at[k, :, pl.ds(pl.multiple_of(ring * ZROWS, ZROWS), ZROWS), :],
                send_sem=fsend.at[k], recv_sem=frecv.at[k], device_id=dev, device_id_type=MESH,
            ).start()

        for i in range(1, 8):
            send_f(i)
        pltpu.make_async_copy(
            fs.at[k, block], p.at[k, :, pl.ds(pl.multiple_of(ring * ZROWS, ZROWS), ZROWS), :], frecv.at[k]
        ).start()

    def stage_g(k):
        drain(p.at[k], frecv.at[k])
        drain(er.at[k], erecv.at[k])
        mirrored = half.astype(F32)

        def one(j, c):
            a = decay(k, j, tab["lz"][...])
            ak = decay(k, j, tab["lk"][...])
            v = p[k, j] * twice(1.0 + mirrored * (tab["sign"][...] - 1.0))
            w = dot_left(tab["bz_i"][...], v)
            outer = [twice(tab["edges"][e]) for e in (2, 3)]
            walls = [twice(tab["walls"][e]) for e in range(2)]
            for t in range(BLOCK):
                v = v * a
                rhs = sq[k, t, j] + w
                for e in range(2):
                    row = jnp.sum(v * outer[e], axis=0, keepdims=True)
                    row = row + er[k, j, pl.ds(2 * t + e, 1), :] + ec[k, j, pl.ds(2 * t + e, 1), :]
                    rhs = rhs + walls[e] * row
                w = ak * rhs
                ws[k, t, j] = dot_left(tab["sine"][...], w)
            return c

        lax.fori_loop(0, KS, one, 0)

        def send_h(one):
            t, y, dev = plane_peer(one)
            pltpu.make_async_remote_copy(
                src_ref=ws.at[k, t, :, pl.ds(pl.multiple_of(y * PLANES, PLANES), PLANES), :],
                dst_ref=s2.at[pl.ds((k * PLACES + place) * KS, KS)],
                send_sem=hsend, recv_sem=hrecv.at[k], device_id=dev, device_id_type=MESH,
            ).start()

        for one in PEERS:
            send_h(one)
        pltpu.make_async_copy(
            ws.at[k, step, :, pl.ds(pl.multiple_of(slab * PLANES, PLANES), PLANES), :],
            s2.at[pl.ds((k * PLACES + place) * KS, KS)],
            hrecv.at[k],
        ).start()

    for k in range(SETS):
        stage_c(k)
        if k > 0:
            stage_e(k - 1)
        if k > 1:
            stage_g(k - 2)
    stage_e(SETS - 1)
    stage_g(SETS - 2)
    stage_g(SETS - 1)

    for k in range(SETS):
        rows = pl.ds(k * PLACES * KS, PLACES * KS)
        drain(s2.at[rows], hrecv.at[k])
        back = dot_right(s2[rows].reshape(PLACES * KS * PLANES, NX), tab["bx_i"][...])
        ty[rows] = back.reshape(PLACES * KS, PLANES, NX)

    @pl.when(last)
    def _():
        drain(u, rsend)

    def store(g):
        return pltpu.make_async_copy(u.at[pl.ds(4 * g, 4)], out_ref.at[0, pl.ds(4 * g, 4)], osem.at[g])

    for g in range(PLANES // 4):
        for i in range(4):
            u[4 * g + i] = dot_left(tab["by_i"][...], ty[:, 4 * g + i, :])
        store(g).start()

    for k in range(SETS):
        drain(s.at[pl.ds(0, 31 * KS)], bsend.at[k])
        drain(p.at[k, :, pl.ds(0, 7 * ZROWS), :], dsend.at[k])
        drain(es.at[k], esend.at[k])
        drain(p.at[k, :, pl.ds(0, 7 * ZROWS), :], fsend.at[k])
    drain(s2.at[pl.ds(0, 31 * ROWS)], hsend)

    @pl.when(helper)
    def _():
        drain(sp.at[pl.ds(0, PLACES - 1)], psend)

    @pl.when(above)
    def _():
        drain(sp.at[0], psend)

    for g in range(PLANES // 4):
        store(g).wait()


def body(iterate, initial):
    dma = pltpu.SemaphoreType.DMA
    vmem = pl.BlockSpec(memory_space=pltpu.VMEM)
    hbm = pl.BlockSpec(memory_space=pl.ANY)
    return pl.pallas_call(
        kernel,
        out_shape=jax.ShapeDtypeStruct(iterate.shape, F32),
        in_specs=[hbm, hbm] + [vmem] * len(NAMES),
        out_specs=hbm,
        scratch_shapes=[
            pltpu.VMEM((PLANES, NY, NX), F32),
            pltpu.VMEM((NY, PLANES, NX), F32),
            pltpu.VMEM((NY, PLANES, NX), F32),
            pltpu.VMEM((HELP, NY, NX), F32),
            pltpu.VMEM((HELP, NY, NX), F32),
            pltpu.VMEM((PLACES, HELP * ROWS, NX), F32),
            pltpu.VMEM((SETS, BLOCK, KS, HALF, NX), F32),
            pltpu.VMEM((PLACES, HELP * ROWS, NX), F32),
            pltpu.VMEM((SETS, BLOCK, KS, HALF, NX), F32),
            pltpu.VMEM((SETS, KS, NZ, NX), F32),
            pltpu.VMEM((SETS, 8, KS, ZROWS, NX), F32),
            pltpu.VMEM((SETS, KS, 2 * BLOCK, NX), F32),
            pltpu.VMEM((SETS, KS, 2 * BLOCK, NX), F32),
            pltpu.VMEM((SETS, KS, 2 * BLOCK, NX), F32),
            pltpu.VMEM((SETS, 4, KS, ZROWS, NX), F32),
            pltpu.VMEM((SETS, KS, NZ, NX), F32),
            pltpu.VMEM((SETS, BLOCK, KS, HALF, NX), F32),
            pltpu.VMEM((NY, PLANES, NX), F32),
            dma, dma, dma((PLANES // 4,)),
            dma((SETS,)), dma((SETS,)), dma, dma, dma, dma,
            dma((SETS,)), dma((SETS,)), dma((SETS,)), dma((SETS,)), dma((SETS,)), dma((SETS,)),
            dma, dma((SETS,)),
        ],
        compiler_params=pltpu.CompilerParams(
            collective_id=0, has_side_effects=True, vmem_limit_bytes=56 * 1024 * 1024
        ),
        cost_estimate=pl.CostEstimate(flops=4 * 10**9, bytes_accessed=6 * 2**20, transcendentals=0),
        name="paradiag",
    )(iterate, initial, *[jnp.asarray(TABLES[n]) for n in NAMES])


def solution(mesh):
    return jax.shard_map(
        body,
        mesh=mesh,
        in_specs=(P("tm", "gz", None, None), P("gz", None, None)),
        out_specs=P("tm", "gz", None, None),
        check_vma=False,
    )
```
